512 devices in a mesh: grp: 8 (over x, z_lo), col: 64 (over y, z_hi, core).
Axes of the slice: x: 4, y: 8, z: 8 (z_hi: 4, z_lo: 2; z = z_hi * 2 + z_lo), core: 2. Of those that a mesh axis runs over, the one named last changes fastest.
Arguments:
- out_grads: bfloat16 [1024, 28672], P('col', 'grp'), may hold values from -1.5 to 1.5
- in_acts: bfloat16 [1024, 8192], P(None, 'col'), may hold values from -1.5 to 1.5
- basis_out: bfloat16 [28672, 24576], P('grp', 'col'), may hold values from -0.03125 to 0.03125
- basis_in: bfloat16 [8192, 8192], P('col', 'grp'), may hold values from -0.0625 to 0.0625
Outputs:
- eigen_fit: float32 [24576, 8192], P('col', 'grp')
The draws below stay inside these ranges and needn't reach their ends.
All inputs are finite; a program needn't handle non-finite values.
Results may differ from the reference program's by a relative error of at most 0.0034.
Values may be sent and summed in bfloat16 or wider, within the bound.
No kernel may reach another device: no remote copies, remote signals or barrier semaphores. Data moves between devices by JAX's collectives and lax.ppermute only.
A program may use at most 64 MiB of HBM per device.

```python
import jax
import jax.numpy as jnp
from jax import lax

D = 8192
FF = 28672
EIG_DEV = 384
T_SIZE = 256
SEQS = 4
TOKENS = 1024
EIG = 24576
N_COL = 64


def block_scale(rng, extent, cuts, smallest, top_value):
    loudness = 1.0
    for axis_at, shards_of in cuts:
        steps = jax.random.uniform(jax.random.fold_in(jax.random.fold_in(rng, 6), axis_at), (shards_of,), jnp.float32, smallest / len(cuts), top_value / len(cuts))
        loudness = loudness * jnp.repeat(jnp.exp(steps), extent[axis_at] // shards_of).reshape((-1,) + (1,) * (len(extent) - 1 - axis_at))
    return loudness


def gaussian(own_key, dims, spread, most, cuts=(), kind=jnp.bfloat16):
    gain = block_scale(own_key, dims, cuts, -0.22, 0.18) if cuts else 1.0
    drawn = jax.random.normal(own_key, dims, jnp.float32) * spread * gain
    return jnp.minimum(jnp.maximum(drawn, -most), most).astype(kind)


def setup_inputs(seed: int = 0) -> dict:
    key_list = jax.random.split(jax.random.key(seed), 5)
    return {
        "out_grads": gaussian(key_list[0], (TOKENS, FF), 0.25, 1.5, ((0, 64), (1, 8))),
        "in_acts": gaussian(key_list[1], (TOKENS, D), 0.25, 1.5, ((1, 64),)),
        "basis_out": gaussian(key_list[2], (FF, EIG), FF ** -0.5, 0.03125, ((0, 8), (1, 64))),
        "basis_in": gaussian(key_list[3], (D, D), D ** -0.5, 0.0625, ((0, 64), (1, 8))),
    }


def reference(out_grads, in_acts, basis_out, basis_in):
    grad_proj = jnp.dot(out_grads, basis_out, preferred_element_type=jnp.float32).astype(jnp.bfloat16)
    act_proj = jnp.dot(in_acts, basis_in, preferred_element_type=jnp.float32).astype(jnp.bfloat16)
    act_seq = act_proj.astype(jnp.float32).reshape(SEQS, T_SIZE, D)
    grad_blocks = grad_proj.astype(jnp.float32).reshape(SEQS, T_SIZE, N_COL, EIG_DEV).transpose(2, 0, 1, 3)

    def fit_block(grad_block):
        blocks = jnp.einsum("sti,stj->sij", grad_block, act_seq)
        return jnp.sum(blocks * blocks, axis=0) / SEQS

    fitted = lax.map(fit_block, grad_blocks)
    return fitted.reshape(N_COL * EIG_DEV, D)
```

```python
import jax
import jax.numpy as jnp
from jax import lax
from jax.sharding import Mesh, PartitionSpec as P

T_SIZE = 256
SEQS = 4
SWAP = [(0, 1), (1, 0)]
F32 = jnp.float32
BF16 = jnp.bfloat16


def dot(a, b):
    return jnp.dot(a, b, preferred_element_type=F32)


def spread(piece, axis, n):
    return lax.all_to_all(jnp.broadcast_to(piece[None], (n,) + piece.shape), axis, 0, 0)


def local(out_grads, in_acts, basis_out, basis_in):
    core = lax.axis_index("core")

    grads = lax.all_gather(out_grads, "zh", axis=0, tiled=True)
    grads = lax.all_gather(grads, "y", axis=0, tiled=True)
    basis_other = lax.ppermute(basis_out, "core", SWAP)

    acts = in_acts.reshape(8, 4, 2, 16, 128).transpose(0, 2, 1, 3, 4).reshape(1024, 128)
    acts = lax.all_gather(acts, "zh", axis=1, tiled=True)
    weights = lax.all_to_all(basis_in, "zh", 1, 0, tiled=True)
    here = lax.dynamic_slice_in_dim(weights, core * 128, 128, 1)
    there = lax.dynamic_slice_in_dim(weights, (1 - core) * 128, 128, 1)
    act = dot(acts, here) + lax.ppermute(dot(acts, there), "core", SWAP)
    act = lax.all_to_all(act.reshape(8, 128, 128), "y", 0, 0)
    act = jnp.sum(act, axis=0).astype(BF16)
    act = spread(act, "y", 8).reshape(1024, 128)
    act = lax.all_gather(act, "zh", axis=0)
    other = lax.ppermute(act, "core", SWAP)
    first = jnp.where(core == 0, act, other)
    second = jnp.where(core == 0, other, act)
    act = jnp.stack([first, second], axis=1)
    act = act.transpose(2, 0, 1, 3).reshape(SEQS, T_SIZE, 1024)

    both = reduce_both(dot(grads, basis_out), dot(grads, basis_other))
    own, sent = both[:, :384], both[:, 384:]
    got = lax.ppermute(sent, "core", SWAP)
    grad = jnp.stack([jnp.where(core == 0, own, got), jnp.where(core == 0, got, own)])
    grad = spread(grad, ("x", "zl"), 8).reshape(SEQS, T_SIZE, 384)

    blocks = jnp.einsum("sti,stj->sij", grad, act, preferred_element_type=F32)
    return jnp.sum(blocks * blocks, axis=0) / SEQS


def reduce_both(mine, others):
    partial = jnp.concatenate([mine, others], axis=1).astype(BF16)
    parts = lax.all_to_all(partial.reshape(8, 64, 768), ("x", "zl"), 0, 0)
    return jnp.sum(parts.astype(F32), axis=0).astype(BF16)


def solution(mesh):
    fine = Mesh(mesh.devices.reshape(4, 2, 8, 4, 2), ("x", "zl", "y", "zh", "core"))
    grp, col = ("x", "zl"), ("y", "zh", "core")
    return jax.shard_map(
        local,
        mesh=fine,
        in_specs=(P(col, grp), P(None, col), P(grp, col), P(col, grp)),
        out_specs=P(col, grp),
        check_vma=False,
    )
```

```python
import jax
import jax.numpy as jnp
from jax import lax
from jax.experimental import pallas as pl
from jax.experimental.pallas import tpu as pltpu
from jax.sharding import Mesh, PartitionSpec as P

SEQS = 4
SWAP = [(0, 1), (1, 0)]
GRP = ("x", "zl")
F32 = jnp.float32
BF16 = jnp.bfloat16
PARAMS = pltpu.CompilerParams(vmem_limit_bytes=40 * 1024 * 1024)


def dot(a, b):
    return jnp.dot(a, b, preferred_element_type=F32)


def exchange(pieces, axis):
    return lax.all_to_all(pieces, axis, 0, 0)


def spread(piece, axis, n):
    return exchange(jnp.broadcast_to(piece[None], (n,) + piece.shape), axis)


def grad_kernel(grads_ref, mine_ref, other_ref, out_ref, acc_ref):
    step = pl.program_id(0)
    mine = dot(grads_ref[...], mine_ref[...])
    other = dot(grads_ref[...], other_ref[...])

    @pl.when(step == 0)
    def _():
        acc_ref[:, :384] = mine
        acc_ref[:, 384:] = other

    @pl.when(step > 0)
    def _():
        acc_ref[:, :384] += mine
        acc_ref[:, 384:] += other

    @pl.when(step == pl.num_programs(0) - 1)
    def _():
        out_ref[...] = acc_ref[...].astype(BF16)


def project_grads(grads, mine, other):
    depth = 512
    return pl.pallas_call(
        grad_kernel,
        grid=(grads.shape[1] // depth,),
        in_specs=[
            pl.BlockSpec((512, depth), lambda k: (0, k)),
            pl.BlockSpec((depth, 384), lambda k: (k, 0)),
            pl.BlockSpec((depth, 384), lambda k: (k, 0)),
        ],
        out_specs=pl.BlockSpec((512, 768), lambda k: (0, 0)),
        out_shape=jax.ShapeDtypeStruct((512, 768), BF16),
        scratch_shapes=[pltpu.VMEM((512, 768), F32)],
        compiler_params=PARAMS,
        name="project_grads",
    )(grads, mine, other)


def act_kernel(core_ref, gathered_ref, here_ref, there_ref):
    core = core_ref[0]
    here = there = None
    for z in range(4):
        acts = gathered_ref[z, :1024, :]
        low = dot(acts, gathered_ref[z, 1024:1152, :])
        high = dot(acts, gathered_ref[z, 1152:1280, :])
        here = low if z == 0 else here + low
        there = high if z == 0 else there + high
    first = core == 0
    here_ref[...] = jnp.where(first, here, there)
    there_ref[...] = jnp.where(first, there, here)


def project_acts(core, gathered):
    half = jax.ShapeDtypeStruct((1024, 128), F32)
    return pl.pallas_call(
        act_kernel,
        in_specs=[
            pl.BlockSpec(memory_space=pltpu.SMEM),
            pl.BlockSpec(memory_space=pltpu.VMEM),
        ],
        out_specs=[pl.BlockSpec(memory_space=pltpu.VMEM)] * 2,
        out_shape=[half, half],
        compiler_params=PARAMS,
        name="project_acts",
    )(core, gathered)


def fit_kernel(core_ref, grad_ref, mine_ref, other_ref, out_ref):
    first = core_ref[0] == 0
    for half in range(2):
        keep = first if half == 0 else jnp.logical_not(first)
        total = None
        for s in range(SEQS):
            mine = mine_ref[2 * s : 2 * s + 2, 0].reshape(256, 128)
            other = other_ref[2 * s : 2 * s + 2, 0].reshape(256, 128)
            act = jnp.where(keep, mine, other)
            grad = grad_ref[256 * s : 256 * s + 256, :]
            block = lax.dot_general(grad, act, (((0,), (0,)), ((), ())), preferred_element_type=F32)
            total = block * block if s == 0 else total + block * block
        out_ref[:, 128 * half : 128 * half + 128] = total * (1.0 / SEQS)


def fit(core, grad, mine, other):
    acts = pl.BlockSpec((8, 1, 128, 128), lambda z: (0, z, 0, 0))
    return pl.pallas_call(
        fit_kernel,
        grid=(4,),
        in_specs=[
            pl.BlockSpec(memory_space=pltpu.SMEM),
            pl.BlockSpec((1024, 384), lambda z: (0, 0)),
            acts,
            acts,
        ],
        out_specs=pl.BlockSpec((384, 256), lambda z: (0, z)),
        out_shape=jax.ShapeDtypeStruct((384, 1024), F32),
        compiler_params=PARAMS,
        name="fit_blocks",
    )(core, grad, mine, other)


def local(out_grads, in_acts, basis_out, basis_in):
    core = lax.axis_index("core")
    core_arr = core.astype(jnp.int32).reshape(1)

    grads = lax.all_gather(out_grads, "zh", axis=0, tiled=True)
    grads, in_acts, basis_out, basis_in = lax.optimization_barrier((grads, in_acts, basis_out, basis_in))
    grads = lax.all_gather(grads, "y", axis=0, tiled=True)
    basis_other = lax.ppermute(basis_out, "core", SWAP)

    halves = basis_in.reshape(128, 8, 128).transpose(1, 0, 2).reshape(4, 256, 128)
    pieces = jnp.concatenate([jnp.broadcast_to(in_acts[None], (4, 1024, 128)), halves], axis=1)
    here, there = project_acts(core_arr, exchange(pieces, "zh"))
    act = here + lax.ppermute(there, "core", SWAP)
    act = jnp.sum(exchange(act.reshape(8, 128, 128), "y"), axis=0).astype(BF16)
    act = act.reshape(4, 2, 16, 128).transpose(1, 0, 2, 3).reshape(128, 128)
    act = spread(act, ("y", "zh"), 32).reshape(8, 4, 128, 128)
    act_other = lax.ppermute(act, "core", SWAP)

    partial = project_grads(grads, basis_out, basis_other)
    parts = exchange(partial.reshape(8, 64, 768), GRP)
    both = jnp.sum(parts.astype(F32), axis=0).astype(BF16)
    own = both[:, :384]
    got = lax.ppermute(both[:, 384:], "core", SWAP)
    grad = jnp.concatenate([jnp.where(core == 0, own, got), jnp.where(core == 0, got, own)])
    grad = spread(grad, GRP, 8).reshape(1024, 384)

    return fit(core_arr, grad, act, act_other)


def solution(mesh):
    fine = Mesh(mesh.devices.reshape(4, 2, 8, 4, 2), ("x", "zl", "y", "zh", "core"))
    col = ("y", "zh", "core")
    return jax.shard_map(
        local,
        mesh=fine,
        in_specs=(P(col, GRP), P(None, col), P(GRP, col), P(col, GRP)),
        out_specs=P(col, GRP),
        check_vma=False,
    )
```

```python
import jax
import jax.numpy as jnp
from jax import lax
from jax.experimental import pallas as pl
from jax.experimental.pallas import tpu as pltpu
from jax.sharding import Mesh, PartitionSpec as P

SEQS = 4
SWAP = [(0, 1), (1, 0)]
GRP = ("x", "zl")
F32 = jnp.float32
BF16 = jnp.bfloat16
VMEM = pl.BlockSpec(memory_space=pltpu.VMEM)
SMEM = pl.BlockSpec(memory_space=pltpu.SMEM)
PARAMS = pltpu.CompilerParams(vmem_limit_bytes=32 * 1024 * 1024)


def dot(a, b):
    return jnp.dot(a, b, preferred_element_type=F32)


def exchange(pieces, axis):
    return lax.all_to_all(pieces, axis, 0, 0)


def spread(piece, axis, n):
    return exchange(jnp.broadcast_to(piece[None], (n,) + piece.shape), axis)


def shift(value, axis, n, by):
    return lax.ppermute(value, axis, [(i, (i + by) % n) for i in range(n)])


def grad_kernel(grads_ref, bases_ref, out_ref, rows_ref, sems):
    depth = 512
    copies = [
        pltpu.make_async_copy(grads_ref.at[:, pl.ds(depth * k, depth)], rows_ref.at[:, pl.ds(depth * k, depth)], sems.at[k])
        for k in range(7)
    ]
    for copy in copies:
        copy.start()
    total = None
    for k in range(7):
        copies[k].wait()
        part = dot(rows_ref[:, depth * k : depth * k + depth], bases_ref[depth * k : depth * k + depth, :256])
        total = part if k == 0 else total + part
    out_ref[:, :256] = total.astype(BF16)
    for n in (256, 512):
        out_ref[:, n : n + 256] = dot(rows_ref[...], bases_ref[:, n : n + 256]).astype(BF16)


def project_grads(grads, bases):
    return pl.pallas_call(
        grad_kernel,
        in_specs=[pl.BlockSpec(memory_space=pltpu.HBM), VMEM],
        out_specs=VMEM,
        out_shape=jax.ShapeDtypeStruct((512, 768), BF16),
        scratch_shapes=[pltpu.VMEM((512, 3584), BF16), pltpu.SemaphoreType.DMA((7,))],
        compiler_params=PARAMS,
        name="project_grads",
    )(grads, bases)


def pieces_kernel(index_ref, acts_ref, weights_ref, out_ref):
    for t in range(2):
        share = acts_ref[pl.ds(pl.multiple_of(512 * t + 64 * index_ref[0], 64), 64), :]
        for q in range(4):
            out_ref[4 * t + q, :64, :] = share
            out_ref[4 * t + q, 64:192, :] = weights_ref[:, 256 * q : 256 * q + 128]
            out_ref[4 * t + q, 192:320, :] = weights_ref[:, 256 * q + 128 : 256 * q + 256]


def make_pieces(index, acts, weights):
    return pl.pallas_call(
        pieces_kernel,
        in_specs=[SMEM, VMEM, VMEM],
        out_specs=VMEM,
        out_shape=jax.ShapeDtypeStruct((8, 320, 128), BF16),
        compiler_params=PARAMS,
        name="make_pieces",
    )(index, acts, weights)


def act_kernel(acts_ref, pieces_ref, out_ref):
    total = None
    for y in range(0, 8, 2):
        acts = jnp.concatenate([acts_ref[:, y].reshape(512, 128), acts_ref[:, y + 1].reshape(512, 128)], axis=1)
        rows = [jnp.concatenate([pieces_ref[y + i, 64:192, :], pieces_ref[y + i, 192:, :]], axis=1) for i in range(2)]
        part = dot(acts, jnp.concatenate(rows, axis=0))
        total = part if y == 0 else total + part
    out_ref[...] = total


def project_acts(acts, pieces):
    return pl.pallas_call(
        act_kernel,
        in_specs=[VMEM, VMEM],
        out_specs=VMEM,
        out_shape=jax.ShapeDtypeStruct((512, 256), F32),
        compiler_params=PARAMS,
        name="project_acts",
    )(acts, pieces)


def fit_kernel(grad_ref, act_ref, out_ref, held_ref, sum_ref, in_sems, out_sems):
    loads = [pltpu.make_async_copy(act_ref.at[y], held_ref.at[y], in_sems.at[y]) for y in range(8)]
    for q in range(4):
        loads[q].start()
        loads[4 + q].start()
    grads = [grad_ref[256 * s : 256 * s + 256, :].T for s in range(SEQS)]
    stores = []
    for q in range(4):
        total = None
        for t in range(2):
            loads[4 * t + q].wait()
            for half in range(2):
                rows = []
                for y in range(2):
                    for parity in range(2):
                        for z in range(4):
                            at = 256 * half + 128 * y + 32 * z + 16 * parity
                            rows.append(held_ref[4 * t + q, at : at + 16, :])
                block = dot(grads[2 * t + half], jnp.concatenate(rows, axis=0))
                total = block * block if total is None else total + block * block
        sum_ref[q] = total * (1.0 / SEQS)
        store = pltpu.make_async_copy(sum_ref.at[q], out_ref.at[:, pl.ds(256 * q, 256)], out_sems.at[q])
        store.start()
        stores.append(store)
    for store in stores:
        store.wait()


def fit(grad, act):
    return pl.pallas_call(
        fit_kernel,
        in_specs=[VMEM, pl.BlockSpec(memory_space=pltpu.HBM)],
        out_specs=pl.BlockSpec(memory_space=pltpu.HBM),
        out_shape=jax.ShapeDtypeStruct((384, 1024), F32),
        scratch_shapes=[
            pltpu.VMEM((8, 512, 256), BF16),
            pltpu.VMEM((4, 384, 256), F32),
            pltpu.SemaphoreType.DMA((8,)),
            pltpu.SemaphoreType.DMA((4,)),
        ],
        compiler_params=PARAMS,
        name="fit_blocks",
    )(grad, act)


def local(out_grads, in_acts, basis_out, basis_in):
    core = lax.axis_index("core")
    group = lax.axis_index(GRP).astype(jnp.int32).reshape(1)

    pieces = make_pieces(group, in_acts, basis_in)
    pieces, out_grads = lax.optimization_barrier((pieces, out_grads))
    pieces = exchange(pieces, "y")

    grads = lax.all_gather(out_grads, "zh", axis=0, tiled=True)
    grads, pieces, basis_out = lax.optimization_barrier((grads, pieces, basis_out))
    grads = lax.all_gather(grads, "y", axis=0, tiled=True)
    basis_other = lax.ppermute(basis_out, "core", SWAP)
    bases = jnp.concatenate([basis_out, basis_other], axis=1)

    acts = spread(pieces[:, :64], GRP, 8)
    acts, bases = lax.optimization_barrier((acts, bases))
    act = project_acts(acts, pieces)
    act = jnp.sum(exchange(act.reshape(8, 64, 256), ("zh", "core")), axis=0).astype(BF16)
    act = spread(act, ("zh", "core"), 8).reshape(512, 256)
    partial = project_grads(grads, bases)
    _, partial = lax.optimization_barrier((act, partial))
    act = lax.all_gather(act, "y", axis=0)

    parts = exchange(partial.reshape(8, 64, 768), GRP)
    both = jnp.sum(parts.astype(F32), axis=0).astype(BF16)
    own, rest = both[:, :384], both[:, 384:]
    pair = jnp.stack([jnp.where(core == 0, own, rest), jnp.where(core == 0, rest, own)])
    pair = jnp.broadcast_to(pair[None], (8, 2, 64, 384)).reshape(16, 64, 384)
    grad = exchange(pair, GRP + ("core",)).reshape(1024, 384)

    return fit(grad, act)


def solution(mesh):
    fine = Mesh(mesh.devices.reshape(4, 2, 8, 4, 2), ("x", "zl", "y", "zh", "core"))
    col = ("y", "zh", "core")
    return jax.shard_map(
        local,
        mesh=fine,
        in_specs=(P(col, GRP), P(None, col), P(GRP, col), P(col, GRP)),
        out_specs=P(col, GRP),
        check_vma=False,
    )
```

```python
import jax
import jax.numpy as jnp
from jax import lax
from jax.experimental import pallas as pl
from jax.experimental.pallas import tpu as pltpu
from jax.sharding import Mesh, PartitionSpec as P

SEQS = 4
SWAP = [(0, 1), (1, 0)]
GRP = ("x", "zl")
F32 = jnp.float32
BF16 = jnp.bfloat16
VMEM = pl.BlockSpec(memory_space=pltpu.VMEM)
SMEM = pl.BlockSpec(memory_space=pltpu.SMEM)
HBM = pl.BlockSpec(memory_space=pltpu.HBM)
ALONE = pltpu.CompilerParams(vmem_limit_bytes=60 * 1024 * 1024)
PARAMS = pltpu.CompilerParams(vmem_limit_bytes=32 * 1024 * 1024)


def dot(a, b):
    return jnp.dot(a, b, preferred_element_type=F32)


def exchange(pieces, axis):
    return lax.all_to_all(pieces, axis, 0, 0)


def spread(piece, axis, n):
    return exchange(jnp.broadcast_to(piece[None], (n,) + piece.shape), axis)


def shift(value, axis, n, by):
    return lax.ppermute(value, axis, [(i, (i + by) % n) for i in range(n)])


def grad_kernel(grads_ref, bases_ref, out_ref, rows_ref, held_ref, sems):
    rows = [pltpu.make_async_copy(grads_ref.at[pl.ds(128 * m, 128)], rows_ref.at[pl.ds(128 * m, 128)], sems.at[m]) for m in range(4)]
    tiles = [pltpu.make_async_copy(bases_ref.at[n], held_ref.at[n], sems.at[4 + n]) for n in range(3)]
    for copy in [tiles[0]] + rows + tiles[1:]:
        copy.start()
    tiles[0].wait()
    for m in range(4):
        rows[m].wait()
        at = slice(128 * m, 128 * m + 128)
        out_ref[at, :256] = dot(rows_ref[at, :], held_ref[0]).astype(BF16)
    for n in (1, 2):
        tiles[n].wait()
        out_ref[:, 256 * n : 256 * n + 256] = dot(rows_ref[...], held_ref[n]).astype(BF16)


def project_grads(grads, bases):
    return pl.pallas_call(
        grad_kernel,
        in_specs=[HBM, HBM],
        out_specs=VMEM,
        out_shape=jax.ShapeDtypeStruct((512, 768), BF16),
        scratch_shapes=[
            pltpu.VMEM((512, 3584), BF16),
            pltpu.VMEM((3, 3584, 256), BF16),
            pltpu.SemaphoreType.DMA((7,)),
        ],
        compiler_params=ALONE,
        name="project_grads",
    )(grads, bases)


def pieces_kernel(index_ref, acts_ref, weights_ref, out_ref, sems):
    copies = []
    for y in range(8):
        t, q = y // 4, y % 4
        share = acts_ref.at[pl.ds(pl.multiple_of(512 * t + 64 * index_ref[0], 64), 64)]
        copies.append(pltpu.make_async_copy(share, out_ref.at[y, pl.ds(0, 64)], sems.at[y]))
        for c in range(2):
            tile = weights_ref.at[:, pl.ds(256 * q + 128 * c, 128)]
            copies.append(pltpu.make_async_copy(tile, out_ref.at[y, pl.ds(64 + 128 * c, 128)], sems.at[8 + 2 * y + c]))
    for copy in copies:
        copy.start()
    for copy in copies:
        copy.wait()


def make_pieces(index, acts, weights):
    return pl.pallas_call(
        pieces_kernel,
        in_specs=[SMEM, HBM, HBM],
        out_specs=VMEM,
        out_shape=jax.ShapeDtypeStruct((8, 320, 128), BF16),
        scratch_shapes=[pltpu.SemaphoreType.DMA((24,))],
        compiler_params=ALONE,
        name="make_pieces",
    )(index, acts, weights)


def act_kernel(acts_ref, pieces_ref, out_ref):
    total = None
    for y in range(0, 8, 2):
        acts = jnp.concatenate([acts_ref[:, y].reshape(512, 128), acts_ref[:, y + 1].reshape(512, 128)], axis=1)
        rows = [jnp.concatenate([pieces_ref[y + i, 64:192, :], pieces_ref[y + i, 192:, :]], axis=1) for i in range(2)]
        part = dot(acts, jnp.concatenate(rows, axis=0))
        total = part if y == 0 else total + part
    out_ref[...] = total


def project_acts(acts, pieces):
    return pl.pallas_call(
        act_kernel,
        in_specs=[VMEM, VMEM],
        out_specs=VMEM,
        out_shape=jax.ShapeDtypeStruct((512, 256), F32),
        compiler_params=PARAMS,
        name="project_acts",
    )(acts, pieces)


def fit_kernel(grad_ref, act_ref, out_ref, sum_ref, sems):
    grads = [grad_ref[256 * s : 256 * s + 256, :].T for s in range(SEQS)]
    stores = []
    for q in range(4):
        total = None
        for s in range(SEQS):
            block = dot(grads[s], act_ref[4 * (s // 2) + q, 256 * (s % 2) : 256 * (s % 2) + 256, :])
            total = block * block if total is None else total + block * block
        sum_ref[q] = total * (1.0 / SEQS)
        store = pltpu.make_async_copy(sum_ref.at[q], out_ref.at[:, pl.ds(256 * q, 256)], sems.at[q])
        store.start()
        stores.append(store)
    for store in stores:
        store.wait()


def fit(grad, act):
    return pl.pallas_call(
        fit_kernel,
        in_specs=[VMEM, VMEM],
        out_specs=HBM,
        out_shape=jax.ShapeDtypeStruct((384, 1024), F32),
        scratch_shapes=[pltpu.VMEM((4, 384, 256), F32), pltpu.SemaphoreType.DMA((4,))],
        compiler_params=PARAMS,
        name="fit_blocks",
    )(grad, act)


def local(out_grads, in_acts, basis_out, basis_in):
    core = lax.axis_index("core")
    group = lax.axis_index(GRP).astype(jnp.int32).reshape(1)

    pieces = make_pieces(group, in_acts, basis_in)
    pieces, out_grads = lax.optimization_barrier((pieces, out_grads))
    pieces = exchange(pieces, "y")

    grads = lax.all_gather(out_grads, "zh", axis=0, tiled=True)
    grads, pieces = lax.optimization_barrier((grads, pieces))
    grads = lax.all_gather(grads, "y", axis=0, tiled=True)
    basis_other = lax.ppermute(basis_out, "core", SWAP)
    middle = jnp.concatenate([basis_out[:, 256:], basis_other[:, :128]], axis=1)
    bases = jnp.stack([basis_out[:, :256], middle, basis_other[:, 128:]])

    acts = spread(pieces[:, :64], GRP, 8)
    acts, bases = lax.optimization_barrier((acts, bases))
    act = project_acts(acts, pieces)
    own = act.reshape(8, 64, 256)
    sums = exchange(own.astype(BF16), ("zh", "core")).astype(F32)
    index = lax.axis_index(("zh", "core"))
    mine = (jnp.arange(8) == index)[:, None, None]
    act = jnp.sum(jnp.where(mine, own, sums), axis=0).astype(BF16)
    act = spread(act, ("zh", "core"), 8).reshape(512, 256)
    partial = project_grads(grads, bases)
    _, partial = lax.optimization_barrier((act, partial))
    act = lax.all_gather(act, "y", axis=0)
    act = act.reshape(8, 4, 4, 2, 16, 256).transpose(0, 1, 3, 2, 4, 5).reshape(8, 512, 256)

    parts = exchange(partial.reshape(8, 64, 768), GRP)
    both = jnp.sum(parts.astype(F32), axis=0).astype(BF16)
    own, rest = both[:, :384], both[:, 384:]
    pair = jnp.stack([jnp.where(core == 0, own, rest), jnp.where(core == 0, rest, own)])
    pair = jnp.broadcast_to(pair[None], (8, 2, 64, 384)).reshape(16, 64, 384)
    grad = exchange(pair, GRP + ("core",)).reshape(1024, 384)

    return fit(grad, act)


def solution(mesh):
    fine = Mesh(mesh.devices.reshape(4, 2, 8, 4, 2), ("x", "zl", "y", "zh", "core"))
    col = ("y", "zh", "core")
    return jax.shard_map(
        local,
        mesh=fine,
        in_specs=(P(col, GRP), P(None, col), P(GRP, col), P(col, GRP)),
        out_specs=P(col, GRP),
        check_vma=False,
    )
```

```python
import jax
import jax.numpy as jnp
from jax import lax
from jax.experimental import pallas as pl
from jax.experimental.pallas import tpu as pltpu
from jax.sharding import Mesh, PartitionSpec as P

SEQS = 4
SWAP = [(0, 1), (1, 0)]
GRP = ("x", "zl")
F32 = jnp.float32
BF16 = jnp.bfloat16
VMEM = pl.BlockSpec(memory_space=pltpu.VMEM)
SMEM = pl.BlockSpec(memory_space=pltpu.SMEM)
HBM = pl.BlockSpec(memory_space=pltpu.HBM)
ALONE = pltpu.CompilerParams(vmem_limit_bytes=60 * 1024 * 1024)
PARAMS = pltpu.CompilerParams(vmem_limit_bytes=32 * 1024 * 1024)


def dot(a, b):
    return jnp.dot(a, b, preferred_element_type=F32)


def exchange(pieces, axis):
    return lax.all_to_all(pieces, axis, 0, 0)


def spread(piece, axis, n):
    return exchange(jnp.broadcast_to(piece[None], (n,) + piece.shape), axis)


def shift(value, axis, n, by):
    return lax.ppermute(value, axis, [(i, (i + by) % n) for i in range(n)])


def grad_kernel(grads_ref, bases_ref, out_ref):
    for n in range(3):
        out_ref[:, 256 * n : 256 * n + 256] = dot(grads_ref[...], bases_ref[n]).astype(BF16)


def project_grads(grads, bases):
    return pl.pallas_call(
        grad_kernel,
        in_specs=[VMEM, VMEM],
        out_specs=VMEM,
        out_shape=jax.ShapeDtypeStruct((512, 768), BF16),
        compiler_params=PARAMS,
        name="project_grads",
    )(grads, bases)


def pieces_kernel(index_ref, acts_ref, weights_ref, out_ref, sems):
    copies = []
    for y in range(8):
        t, q = y // 4, y % 4
        share = acts_ref.at[pl.ds(pl.multiple_of(512 * t + 64 * index_ref[0], 64), 64)]
        copies.append(pltpu.make_async_copy(share, out_ref.at[y, pl.ds(0, 64)], sems.at[y]))
        for c in range(2):
            tile = weights_ref.at[:, pl.ds(256 * q + 128 * c, 128)]
            copies.append(pltpu.make_async_copy(tile, out_ref.at[y, pl.ds(64 + 128 * c, 128)], sems.at[8 + 2 * y + c]))
    for copy in copies:
        copy.start()
    for copy in copies:
        copy.wait()


def make_pieces(index, acts, weights):
    return pl.pallas_call(
        pieces_kernel,
        in_specs=[SMEM, HBM, HBM],
        out_specs=VMEM,
        out_shape=jax.ShapeDtypeStruct((8, 320, 128), BF16),
        scratch_shapes=[pltpu.SemaphoreType.DMA((24,))],
        compiler_params=ALONE,
        name="make_pieces",
    )(index, acts, weights)


def act_kernel(core_ref, acts_ref, pieces_ref, here_ref, there_ref):
    total = None
    for y in range(0, 8, 2):
        acts = jnp.concatenate([acts_ref[:, y].reshape(512, 128), acts_ref[:, y + 1].reshape(512, 128)], axis=1)
        rows = [jnp.concatenate([pieces_ref[y + i, 64:192, :], pieces_ref[y + i, 192:, :]], axis=1) for i in range(2)]
        part = dot(acts, jnp.concatenate(rows, axis=0))
        total = part if y == 0 else total + part
    first = core_ref[0] == 0
    here_ref[...] = jnp.where(first, total[:256], total[256:])
    there_ref[...] = jnp.where(first, total[256:], total[:256])


def project_acts(core, acts, pieces):
    half = jax.ShapeDtypeStruct((256, 256), F32)
    return pl.pallas_call(
        act_kernel,
        in_specs=[SMEM, VMEM, VMEM],
        out_specs=[VMEM, VMEM],
        out_shape=[half, half],
        compiler_params=PARAMS,
        name="project_acts",
    )(core, acts, pieces)


def fit_kernel(grad_ref, act_ref, out_ref, sum_ref, sems):
    grads = [grad_ref[256 * s : 256 * s + 256, :].T for s in range(SEQS)]
    stores = []
    for q in range(4):
        total = None
        for s in range(SEQS):
            block = dot(grads[s], act_ref[4 * (s // 2) + q, 256 * (s % 2) : 256 * (s % 2) + 256, :])
            total = block * block if total is None else total + block * block
        sum_ref[q] = total * (1.0 / SEQS)
        store = pltpu.make_async_copy(sum_ref.at[q], out_ref.at[:, pl.ds(256 * q, 256)], sems.at[q])
        store.start()
        stores.append(store)
    for store in stores:
        store.wait()


def fit(grad, act):
    return pl.pallas_call(
        fit_kernel,
        in_specs=[VMEM, VMEM],
        out_specs=HBM,
        out_shape=jax.ShapeDtypeStruct((384, 1024), F32),
        scratch_shapes=[pltpu.VMEM((4, 384, 256), F32), pltpu.SemaphoreType.DMA((4,))],
        compiler_params=PARAMS,
        name="fit_blocks",
    )(grad, act)


def local(out_grads, in_acts, basis_out, basis_in):
    core = lax.axis_index("core")
    group = lax.axis_index(GRP).astype(jnp.int32).reshape(1)

    pieces = make_pieces(group, in_acts, basis_in)
    pieces, out_grads = lax.optimization_barrier((pieces, out_grads))
    pieces = exchange(pieces, "y")

    grads = lax.all_gather(out_grads, "zh", axis=0, tiled=True)
    grads, pieces, basis_out = lax.optimization_barrier((grads, pieces, basis_out))
    grads = lax.all_gather(grads, "y", axis=0, tiled=True)
    basis_other = lax.ppermute(basis_out, "core", SWAP)
    middle = jnp.concatenate([basis_out[:, 256:], basis_other[:, :128]], axis=1)
    bases = jnp.stack([basis_out[:, :256], middle, basis_other[:, 128:]])

    acts = spread(pieces[:, :64], GRP, 8)
    here, there = project_acts(core.astype(jnp.int32).reshape(1), acts, pieces)
    own = here + lax.ppermute(there, "core", SWAP)
    sums = spread(own.astype(BF16), "zh", 4)
    sums, bases = lax.optimization_barrier((sums, bases))
    mine = (jnp.arange(4) == lax.axis_index("zh"))[:, None, None]
    act = jnp.sum(jnp.where(mine, own[None], sums.astype(F32)), axis=0).astype(BF16)
    other = lax.ppermute(act, "core", SWAP)
    act = jnp.concatenate([jnp.where(core == 0, act, other), jnp.where(core == 0, other, act)])
    partial = project_grads(grads, bases)
    _, partial = lax.optimization_barrier((act, partial))
    act = lax.all_gather(act, "y", axis=0)
    act = act.reshape(8, 4, 4, 2, 16, 256).transpose(0, 1, 3, 2, 4, 5).reshape(8, 512, 256)

    parts = exchange(partial.reshape(8, 64, 768), GRP)
    both = jnp.sum(parts.astype(F32), axis=0).astype(BF16)
    own, rest = both[:, :384], both[:, 384:]
    pair = jnp.stack([jnp.where(core == 0, own, rest), jnp.where(core == 0, rest, own)])
    pair = jnp.broadcast_to(pair[None], (8, 2, 64, 384)).reshape(16, 64, 384)
    grad = exchange(pair, GRP + ("core",)).reshape(1024, 384)

    return fit(grad, act)


def solution(mesh):
    fine = Mesh(mesh.devices.reshape(4, 2, 8, 4, 2), ("x", "zl", "y", "zh", "core"))
    col = ("y", "zh", "core")
    return jax.shard_map(
        local,
        mesh=fine,
        in_specs=(P(col, GRP), P(None, col), P(GRP, col), P(col, GRP)),
        out_specs=P(col, GRP),
        check_vma=False,
    )
```

```python
import jax
import jax.numpy as jnp
from jax import lax
from jax.experimental import pallas as pl
from jax.experimental.pallas import tpu as pltpu
from jax.sharding import Mesh, PartitionSpec as P

SEQS = 4
SWAP = [(0, 1), (1, 0)]
GRP = ("x", "zl")
F32 = jnp.float32
BF16 = jnp.bfloat16
VMEM = pl.BlockSpec(memory_space=pltpu.VMEM)
SMEM = pl.BlockSpec(memory_space=pltpu.SMEM)
HBM = pl.BlockSpec(memory_space=pltpu.HBM)
ALONE = pltpu.CompilerParams(vmem_limit_bytes=60 * 1024 * 1024)
PARAMS = pltpu.CompilerParams(vmem_limit_bytes=32 * 1024 * 1024)


def dot(a, b):
    return jnp.dot(a, b, preferred_element_type=F32)


def exchange(pieces, axis):
    return lax.all_to_all(pieces, axis, 0, 0)


def spread(piece, axis, n):
    return exchange(jnp.broadcast_to(piece[None], (n,) + piece.shape), axis)


def shift(value, axis, n, by):
    return lax.ppermute(value, axis, [(i, (i + by) % n) for i in range(n)])


def grad_kernel(grads_ref, bases_ref, out_ref):
    for n in range(3):
        out_ref[:, 256 * n : 256 * n + 256] = dot(grads_ref[...], bases_ref[n]).astype(BF16)


def project_grads(grads, bases):
    return pl.pallas_call(
        grad_kernel,
        in_specs=[VMEM, VMEM],
        out_specs=VMEM,
        out_shape=jax.ShapeDtypeStruct((512, 768), BF16),
        compiler_params=PARAMS,
        name="project_grads",
    )(grads, bases)


def join_kernel(mine_ref, other_ref, out_ref):
    out_ref[0] = mine_ref[:, :256]
    out_ref[1, :, :128] = mine_ref[:, 256:]
    out_ref[1, :, 128:] = other_ref[:, :128]
    out_ref[2] = other_ref[:, 128:]


def join(mine, other):
    return pl.pallas_call(
        join_kernel,
        in_specs=[VMEM, VMEM],
        out_specs=VMEM,
        out_shape=jax.ShapeDtypeStruct((3, 3584, 256), BF16),
        compiler_params=PARAMS,
        name="join_bases",
    )(mine, other)


def pieces_kernel(index_ref, acts_ref, weights_ref, out_ref, sems):
    copies = []
    for y in range(8):
        t, q = y // 4, y % 4
        share = acts_ref.at[pl.ds(pl.multiple_of(512 * t + 64 * index_ref[0], 64), 64)]
        copies.append(pltpu.make_async_copy(share, out_ref.at[y, pl.ds(0, 64)], sems.at[y]))
        for c in range(2):
            tile = weights_ref.at[:, pl.ds(256 * q + 128 * c, 128)]
            copies.append(pltpu.make_async_copy(tile, out_ref.at[y, pl.ds(64 + 128 * c, 128)], sems.at[8 + 2 * y + c]))
    for copy in copies:
        copy.start()
    for copy in copies:
        copy.wait()


def make_pieces(index, acts, weights):
    return pl.pallas_call(
        pieces_kernel,
        in_specs=[SMEM, HBM, HBM],
        out_specs=VMEM,
        out_shape=jax.ShapeDtypeStruct((8, 320, 128), BF16),
        scratch_shapes=[pltpu.SemaphoreType.DMA((24,))],
        compiler_params=ALONE,
        name="make_pieces",
    )(index, acts, weights)


def act_kernel(core_ref, acts_ref, pieces_ref, here_ref, there_ref):
    total = None
    for y in range(0, 8, 2):
        acts = jnp.concatenate([acts_ref[:, y].reshape(512, 128), acts_ref[:, y + 1].reshape(512, 128)], axis=1)
        rows = [jnp.concatenate([pieces_ref[y + i, 64:192, :], pieces_ref[y + i, 192:, :]], axis=1) for i in range(2)]
        part = dot(acts, jnp.concatenate(rows, axis=0))
        total = part if y == 0 else total + part
    first = core_ref[0] == 0
    here_ref[...] = jnp.where(first, total[:256], total[256:])
    there_ref[...] = jnp.where(first, total[256:], total[:256])


def project_acts(core, acts, pieces):
    half = jax.ShapeDtypeStruct((256, 256), F32)
    return pl.pallas_call(
        act_kernel,
        in_specs=[SMEM, VMEM, VMEM],
        out_specs=[VMEM, VMEM],
        out_shape=[half, half],
        compiler_params=PARAMS,
        name="project_acts",
    )(core, acts, pieces)


def fit_kernel(grad_ref, act_ref, out_ref, sum_ref, sems):
    grads = [grad_ref[256 * s : 256 * s + 256, :].T for s in range(SEQS)]
    stores = []
    for q in range(4):
        total = None
        for s in range(SEQS):
            block = dot(grads[s], act_ref[4 * (s // 2) + q, 256 * (s % 2) : 256 * (s % 2) + 256, :])
            total = block * block if total is None else total + block * block
        sum_ref[q] = total * (1.0 / SEQS)
        store = pltpu.make_async_copy(sum_ref.at[q], out_ref.at[:, pl.ds(256 * q, 256)], sems.at[q])
        store.start()
        stores.append(store)
    for store in stores:
        store.wait()


def fit(grad, act):
    return pl.pallas_call(
        fit_kernel,
        in_specs=[VMEM, VMEM],
        out_specs=HBM,
        out_shape=jax.ShapeDtypeStruct((384, 1024), F32),
        scratch_shapes=[pltpu.VMEM((4, 384, 256), F32), pltpu.SemaphoreType.DMA((4,))],
        compiler_params=PARAMS,
        name="fit_blocks",
    )(grad, act)


def local(out_grads, in_acts, basis_out, basis_in):
    core = lax.axis_index("core")
    group = lax.axis_index(GRP).astype(jnp.int32).reshape(1)

    pieces = make_pieces(group, in_acts, basis_in)
    pieces, out_grads = lax.optimization_barrier((pieces, out_grads))
    pieces = exchange(pieces, "y")

    grads = lax.all_gather(out_grads, "zh", axis=0, tiled=True)
    grads, pieces, basis_out = lax.optimization_barrier((grads, pieces, basis_out))
    grads = lax.all_gather(grads, "y", axis=0, tiled=True)
    basis_other = lax.ppermute(basis_out, "core", SWAP)
    bases = join(basis_out, basis_other)

    acts = spread(pieces[:, :64], GRP, 8)
    here, there = project_acts(core.astype(jnp.int32).reshape(1), acts, pieces)
    own = here + lax.ppermute(there, "core", SWAP)
    sums = spread(own.astype(BF16), "zh", 4)
    sums, bases = lax.optimization_barrier((sums, bases))
    mine = (jnp.arange(4) == lax.axis_index("zh"))[:, None, None]
    act = jnp.sum(jnp.where(mine, own[None], sums.astype(F32)), axis=0).astype(BF16)
    other = lax.ppermute(act, "core", SWAP)
    act = jnp.concatenate([jnp.where(core == 0, act, other), jnp.where(core == 0, other, act)])
    partial = project_grads(grads, bases)
    _, partial = lax.optimization_barrier((act, partial))
    act = lax.all_gather(act, "y", axis=0)
    act = act.reshape(8, 4, 4, 2, 16, 256).transpose(0, 1, 3, 2, 4, 5).reshape(8, 512, 256)

    parts = exchange(partial.reshape(8, 64, 768), GRP)
    both = jnp.sum(parts.astype(F32), axis=0).astype(BF16)
    own, rest = both[:, :384], both[:, 384:]
    pair = jnp.stack([jnp.where(core == 0, own, rest), jnp.where(core == 0, rest, own)])
    pair = jnp.broadcast_to(pair[None], (8, 2, 64, 384)).reshape(16, 64, 384)
    grad = exchange(pair, GRP + ("core",)).reshape(1024, 384)

    return fit(grad, act)


def solution(mesh):
    fine = Mesh(mesh.devices.reshape(4, 2, 8, 4, 2), ("x", "zl", "y", "zh", "core"))
    col = ("y", "zh", "core")
    return jax.shard_map(
        local,
        mesh=fine,
        in_specs=(P(col, GRP), P(None, col), P(GRP, col), P(col, GRP)),
        out_specs=P(col, GRP),
        check_vma=False,
    )
```
